256 devices in a mesh: chan: 32 (over x, y, z_lo), tm: 8 (over z_hi, core).
Axes of the slice: x: 4, y: 4, z: 8 (z_hi: 4, z_lo: 2; z = z_hi * 2 + z_lo), core: 2. Of those that a mesh axis runs over, the one named last changes fastest.
Arguments:
- voltages: bfloat16 [2, 2048, 256, 1024], P(None, 'chan', None, 'tm'), may hold values from -7 to 7, as said below
- channel_gains: float32 [2, 2048, 256], P(None, 'chan'), may hold values from -1.5 to 1.5
- weights: bfloat16 [2, 256, 256, 2048], P(None, 'chan', None, 'tm'), may hold values from -0.09375 to 0.09375
- scales: float32 [256], P('chan'), may hold values from 0.5 to 2
- fir_taps: int32 [4, 16], replicated, may hold values from 1 to 16
Outputs:
- formed_beams: float32 [2, 256, 64, 16, 256], P(None, 'chan', 'tm')
The draws below stay inside these ranges and needn't reach their ends.
Inputs may be any that keep to these rules, and one draw needn't show every extreme that they name: voltages hold whole numbers.
All inputs are finite; a program needn't handle non-finite values.
Results may differ from the reference program's by a relative error of at most 0.0041.
Values may be sent and summed in bfloat16 or wider, within the bound.
A program may use at most 192 MiB of HBM per device.

```python
import math
import jax
import jax.numpy as jnp
from jax import lax

INPUTS = 2048
CHAN = 256
BEAMS = 256
UPCH = 16
TAPS = 4
SAMPLES = 1024
FRAMES = 64


def draw_voltages(key, part):
    values = jax.random.randint(key, (2, INPUTS, CHAN, SAMPLES), -7, 8)
    return values.astype(jnp.float32).astype(jnp.bfloat16)


def plant(entries, own_key, least, largest):
    spot = [jax.random.randint(jax.random.fold_in(own_key, axis), (), 0, length) for axis, length in enumerate(entries.shape)]
    main_axis = entries.shape.index(max(entries.shape))
    next_to = spot[:main_axis] + [(spot[main_axis] + 1) % entries.shape[main_axis]] + spot[main_axis + 1:]
    return entries.at[tuple(spot)].set(least).at[tuple(next_to)].set(largest)


def level_of(key, extent, pieces, least, high):
    level, own = 1.0, jax.random.fold_in(key, 6)
    for axis_at, parts in pieces:
        heights = jnp.exp(jax.random.uniform(jax.random.fold_in(own, axis_at), (parts,), jnp.float32, least / len(pieces), high / len(pieces)))
        level = level * jnp.repeat(heights, extent[axis_at] // parts).reshape([-1 if axis == axis_at else 1 for axis in range(len(extent))])
    return level


def bell_draw(own_key, extent, width, limit, cuts=(), kind=jnp.bfloat16):
    values = width * jax.random.normal(own_key, extent, jnp.float32)
    if cuts:
        values = values * level_of(own_key, extent, cuts, -0.22, 0.18)
    return jnp.clip(values, -limit, limit).astype(kind)


def setup_inputs(seed: int = 0) -> dict:
    arg_keys = jax.random.split(jax.random.key(seed), 6)
    return {
        "voltages": draw_voltages(jax.random.fold_in(arg_keys[5], 71), 0),
        "channel_gains": bell_draw(arg_keys[1], (2, INPUTS, CHAN), 0.25, 1.5, ((1, 32),), jnp.float32),
        "weights": bell_draw(arg_keys[2], (2, CHAN, BEAMS, INPUTS), (2 * INPUTS) ** -0.5, 0.09375, ((1, 32), (3, 8))),
        "scales": jnp.clip(jnp.exp(math.log(2.0) - 1.3862944 * jax.random.uniform(arg_keys[3], (CHAN,), jnp.float32) ** level_of(arg_keys[3], (CHAN,), ((0, 32),), -0.2, 0.2)), 0.5, 2.0),
        "fir_taps": plant(jax.random.randint(arg_keys[4], (TAPS, UPCH), 1, 17), jax.random.fold_in(arg_keys[4], 1), 1, 16).astype(jnp.int32),
    }


def dft_tables(length):
    positions = jnp.arange(length, dtype=jnp.int32)
    product = positions[:, None] * positions[None, :] % length
    phase_angle = product.astype(jnp.float32) * (2.0 * math.pi / length)
    return (jnp.cos(phase_angle), jnp.sin(phase_angle))

def calibrate(voltage, gain_col):
    volt_re = voltage[0].astype(jnp.float32)
    volt_im = voltage[1].astype(jnp.float32)
    gain_re = gain_col[0][..., None]
    gain_im = gain_col[1][..., None]
    return jnp.stack([gain_re * volt_re - gain_im * volt_im, gain_re * volt_im + gain_im * volt_re]).astype(jnp.bfloat16)

def channelize(extended, fir_taps):
    tap_count, length = fir_taps.shape
    leading = extended.shape[:-1]
    frames = extended.shape[-1] // length - (tap_count - 1)
    blocks = extended.astype(jnp.float32).reshape(leading + (frames + tap_count - 1, length))
    tap_coef = fir_taps.astype(jnp.float32) / 16.0
    filtered = tap_coef[0] * blocks[..., tap_count - 1:tap_count - 1 + frames, :]
    for tap_index in range(1, tap_count):
        begin_at = tap_count - 1 - tap_index
        filtered = filtered + tap_coef[tap_index] * blocks[..., begin_at:begin_at + frames, :]
    cosine_table, sine_table = dft_tables(length)
    dft_norm = 1.0 / math.sqrt(length)
    highest = lax.Precision.HIGHEST
    real_part = (jnp.einsum('...k,gk->...g', filtered[0], cosine_table, precision=highest) + jnp.einsum('...k,gk->...g', filtered[1], sine_table, precision=highest)) * dft_norm
    imag_part = (jnp.einsum('...k,gk->...g', filtered[1], cosine_table, precision=highest) - jnp.einsum('...k,gk->...g', filtered[0], sine_table, precision=highest)) * dft_norm
    return jnp.stack([real_part, imag_part]).astype(jnp.bfloat16)

def arrange(spectra):
    moved = jnp.transpose(spectra, (2, 3, 4, 0, 1))
    return moved.reshape(moved.shape[0], moved.shape[1] * moved.shape[2], 2, moved.shape[4])

def beam_exact(spectra, weight):
    weight_re = weight[0].astype(jnp.float32)
    weight_im = weight[1].astype(jnp.float32)
    row_re = jnp.stack([weight_re, -weight_im], axis=2)
    row_im = jnp.stack([weight_im, weight_re], axis=2)
    panel_all = jnp.concatenate([row_re, row_im], axis=1)
    return jnp.einsum('cnpx,cypx->cny', spectra.astype(jnp.float32), panel_all, precision=lax.Precision.HIGHEST)

def reference(voltages, channel_gains, weights, scales, fir_taps):
    halo_len = (TAPS - 1) * UPCH

    def per_channel(channel):
        voltage = lax.dynamic_slice_in_dim(voltages, channel, 1, 2)
        gain_col = lax.dynamic_slice_in_dim(channel_gains, channel, 1, 2)
        panel_one = lax.dynamic_slice_in_dim(weights, channel, 1, 1)
        scale_one = lax.dynamic_slice_in_dim(scales, channel, 1, 0)
        calibrated = calibrate(voltage, gain_col)
        zero_lead = jnp.zeros(calibrated.shape[:-1] + (halo_len,), jnp.bfloat16)
        spectra = arrange(channelize(jnp.concatenate([zero_lead, calibrated], axis=-1), fir_taps))
        beam_sums = beam_exact(spectra, panel_one)
        return beam_sums[0] * scale_one[0]
    channels = jnp.arange(CHAN, dtype=jnp.int32)
    formed = lax.map(per_channel, channels)
    formed = formed.reshape(CHAN, FRAMES, UPCH, 2, BEAMS)
    return jnp.transpose(formed, (3, 0, 1, 2, 4))
```

```python
import math

import jax
import jax.numpy as jnp
import numpy as np
from jax import lax
from jax.experimental import pallas as pl
from jax.experimental.pallas import tpu as pltpu
from jax.sharding import PartitionSpec as P

MESH = pl.DeviceIdType.MESH
F32 = jnp.float32
BF16 = jnp.bfloat16
NT = (((1,), (1,)), ((), ()))

INPUTS_HERE = 64
GROUP = 8
SPAN = 128
BEAMS = 256
LENGTH = 16
SPILL = 48
ROWS = 4 * SPAN + 2 * SPILL


def channelizer(fir_taps):
    sample = np.arange(SPAN)
    row = np.arange(SPAN + SPILL)
    lag = row[:, None] // LENGTH - sample[None, :] // LENGTH
    turn = (row[:, None] % LENGTH) * (sample[None, :] % LENGTH) % LENGTH
    angle = turn * (2.0 * math.pi / LENGTH)
    norm = 1.0 / (16.0 * math.sqrt(LENGTH))
    cos = jnp.asarray((np.cos(angle) * norm).astype(np.float32))
    sin = jnp.asarray((np.sin(angle) * norm).astype(np.float32))
    taps = jnp.tile(fir_taps.astype(F32), (1, SPAN // LENGTH))
    weight = jnp.zeros((SPAN + SPILL, SPAN), F32)
    for tap in range(fir_taps.shape[0]):
        weight = jnp.where(jnp.asarray(lag == tap), taps[tap][None, :], weight)
    cos, sin = cos * weight, sin * weight
    re = jnp.concatenate([cos, sin], axis=1)
    im = jnp.concatenate([-sin, cos], axis=1)
    full = jnp.concatenate([re[:SPAN], im[:SPAN], re[SPAN:], im[SPAN:]], axis=0)
    high = lax.reduce_precision(full, 8, 7)
    return jnp.concatenate([high, full - high], axis=0).astype(BF16)


def parity_split():
    q = np.arange(256)
    source = (q % 128) // 64 * 128 + (q // 128) * 64 + q % 64
    return jnp.asarray((np.arange(256)[:, None] == source[None, :]).astype(np.float32)).astype(BF16)


def kernel(
    v_ref, g_ref, w_ref, ct_ref, perm_ref, sc_ref, o_ref,
    vbuf, gbuf, wsplit, wbuf, spec, vf, xbuf, spf, osend, obuf, ssend, sbuf,
    v_send, v_recv, g_send, g_recv, w_send, w_recv, f_send, o_send, o_recv, s_send, s_recv,
):
    chan, tm = lax.axis_index("chan"), lax.axis_index("tm")
    xy, z = lax.div(chan, 2), lax.rem(chan, 2)
    t, k = lax.div(tm, 2), lax.rem(tm, 2)
    x, y = lax.div(xy, 4), lax.rem(xy, 4)
    u = lax.div(y, 2)
    differ = lax.rem(z + k, 2)

    def remote(src, dst, send, recv, to_chan, to_tm):
        return pltpu.make_async_remote_copy(
            src_ref=src, dst_ref=dst, send_sem=send, recv_sem=recv,
            device_id=(to_chan, to_tm), device_id_type=MESH,
        )

    def arrived(ref, sem):
        pltpu.make_async_copy(ref, ref, sem).wait()

    barrier = pltpu.get_barrier_semaphore()

    @pl.loop(1, 32)
    def _(n):
        other = lax.rem(xy * 2 + k + n, 32)
        pl.semaphore_signal(
            barrier, inc=1, device_id=(lax.div(other, 2) * 2 + z, t * 2 + lax.rem(other, 2)), device_id_type=MESH
        )

    @pl.loop(2, 16)
    def _(n):
        there = lax.rem(t * 2 + z + lax.div(n, 2), 8)
        pl.semaphore_signal(
            barrier, inc=1, device_id=(xy * 2 + lax.rem(there, 2), lax.div(there, 2) * 2 + lax.rem(n, 2)), device_id_type=MESH
        )

    pl.semaphore_wait(barrier, 31 + 14)

    def offsets(p):
        a = lax.div(p, 2)
        return a + lax.div(a, 2) - 2 * lax.div(a, 3), lax.rem(p, 2)

    def v_copies(p, e, k2):
        dx, du = offsets(p)
        to_xy = lax.rem(x - dx + 4, 4) * 4 + lax.rem(u + du, 2) * 2 + e
        group = to_xy * 2 + k2
        local = jnp.logical_and(to_xy == xy, k2 == k)
        far = remote(
            v_ref.at[:, :, group], vbuf.at[xy, k], v_send.at[group], v_recv.at[xy * 2 + k], to_xy * 2 + z, t * 2 + k2
        )
        near = pltpu.make_async_copy(v_ref.at[:, :, group], vbuf.at[xy, k], v_recv.at[xy * 2 + k])
        return local, far, near

    def g_copies(p, e):
        dx, du = offsets(p)
        to_xy = lax.rem(x - dx + 4, 4) * 4 + lax.rem(u + du, 2) * 2 + e
        far = remote(g_ref.at[to_xy * 2 + k], gbuf.at[xy], g_send.at[to_xy], g_recv.at[xy], to_xy * 2 + z, tm)
        near = pltpu.make_async_copy(g_ref.at[to_xy * 2 + k], gbuf.at[xy], g_recv.at[xy])
        return to_xy == xy, far, near

    def w_columns(slot):
        return pl.ds(pl.multiple_of(slot * 128, 128), 128)

    def w_copies(c):
        dst = wbuf.at[c, :, w_columns(tm)]
        sem = w_recv.at[c * 8 + tm]
        mine, others = wsplit.at[z, c], wsplit.at[1 - z, c]
        over = xy * 2 + 1 - z
        near = pltpu.make_async_copy(mine, dst, sem)
        sibling = remote(mine, dst, w_send.at[c * 5], sem, chan, t * 2 + z)
        far = [
            remote(others, dst, w_send.at[c * 5 + 1], sem, over, lax.rem(t + z, 4) * 2 + z),
            remote(others, dst, w_send.at[c * 5 + 2], sem, over, lax.rem(t + z + 3, 4) * 2 + z),
            remote(mine, dst, w_send.at[c * 5 + 3], sem, chan, lax.rem(t + 1, 4) * 2 + z),
            remote(mine, dst, w_send.at[c * 5 + 4], sem, chan, lax.rem(t + 3, 4) * 2 + z),
        ]
        return near, sibling, far

    behind = lax.rem(t + 3 + differ * z, 4)
    ahead = lax.rem(t + 1 - differ + differ * z, 4)

    def forward(c, slot, index, step):
        block = wbuf.at[c, :, w_columns(slot)]
        return remote(
            block, block, f_send.at[c * 4 + index], w_recv.at[c * 8 + slot], chan, lax.rem(t + 4 + step, 4) * 2 + k
        )

    def forwards(c):
        always = [forward(c, behind * 2, 0, 1), forward(c, ahead * 2 + 1, 1, -1)]
        crossed = [forward(c, behind * 2 + 1, 2, 1), forward(c, ahead * 2, 3, -1)]
        return always, crossed

    @pl.loop(0, 8)
    def _(c):
        both = jnp.concatenate([w_ref[0, c], w_ref[1, c]], axis=0)
        split = jnp.dot(both, perm_ref[...], preferred_element_type=F32).astype(BF16)
        wsplit[0, c] = split[:, :128]
        wsplit[1, c] = split[:, 128:]
        near, sibling, far = w_copies(c)
        for copy in far:
            copy.start()

        @pl.when(differ == 0)
        def _():
            near.start()

        @pl.when(differ == 1)
        def _():
            sibling.start()

        for e in range(2):
            here, far, near = g_copies(c, e)
            pl.when(here)(near.start)
            pl.when(jnp.logical_not(here))(far.start)
            for k2 in range(2):
                here, far, near = v_copies(c, e, k2)
                pl.when(here)(near.start)
                pl.when(jnp.logical_not(here))(far.start)

    @pl.loop(0, 8)
    def _(p):
        for slot in (behind * 2, behind * 2 + 1, ahead * 2, ahead * 2 + 1):
            arrived(wbuf.at[p, :, w_columns(slot)], w_recv.at[p * 8 + slot])
        always, crossed = forwards(p)
        for copy in always:
            copy.start()

        @pl.when(differ == 1)
        def _():
            for copy in crossed:
                copy.start()

        dx, du = offsets(p)
        pair = lax.rem(x + dx, 4) * 2 + lax.rem(u + du, 2)
        for e in range(2):
            arrived(gbuf.at[pair * 2 + e], g_recv.at[pair * 2 + e])
            for half in range(2):
                arrived(vbuf.at[pair * 2 + e, half], v_recv.at[pair * 4 + 2 * e + half])
        turned = [gbuf[pair * 2 + e].T for e in range(2)]
        gain_re = jnp.concatenate([turned[e][:64] for e in range(2)], axis=0)
        gain_im = jnp.concatenate([turned[e][64:] for e in range(2)], axis=0)
        columns = pl.ds(pl.multiple_of(pair * 128, 128), 128)
        for half in range(2):
            for part in range(2):
                for e in range(2):
                    vf[part, e * 512 : (e + 1) * 512] = (
                        vbuf[pair * 2 + e, half, part].astype(F32).reshape(512, 128)
                    )
            for c in range(8):
                volt_re, volt_im = (
                    jnp.concatenate(
                        [vf.at[part][pl.ds(e * 512 + c, 64, stride=8), :] for e in range(2)], axis=0
                    )
                    for part in range(2)
                )
                g_re, g_im = gain_re[:, c : c + 1], gain_im[:, c : c + 1]
                xbuf[c * 128 : (c + 1) * 128, :128] = (g_re * volt_re - g_im * volt_im).astype(BF16)
                xbuf[c * 128 : (c + 1) * 128, 128:] = (g_re * volt_im + g_im * volt_re).astype(BF16)

            @pl.loop(0, 4)
            def _(q):
                rows = xbuf[pl.ds(pl.multiple_of(q * 256, 256), 256)]
                made = lax.dot_general(ct_ref[...], rows, NT, preferred_element_type=F32)
                made = made[:352] + made[352:]
                re, im, tail = made[:128], made[128:256], made[256:]
                if half == 0:
                    spf[q] = tail
                else:
                    before = spf[q]
                    re = jnp.concatenate([re[:SPILL] + before[:SPILL], re[SPILL:]], axis=0)
                    im = jnp.concatenate([im[:SPILL] + before[SPILL:], im[SPILL:]], axis=0)
                for d in range(2):
                    lanes = slice(d * 128, (d + 1) * 128)
                    spec[q * 2 + d, half * 128 : half * 128 + 128, columns] = re[:, lanes].astype(BF16)
                    spec[q * 2 + d, 256 + half * 128 : 384 + half * 128, columns] = im[:, lanes].astype(BF16)
                    if half == 1:
                        spec[q * 2 + d, 512:ROWS, columns] = tail[:, lanes].astype(BF16)

    def o_copies(c, half):
        src, dst, sem = osend.at[c, half], obuf.at[c, z], o_recv.at[c * 2 + z]
        near = pltpu.make_async_copy(src, dst, sem)
        far = remote(src, dst, o_send.at[c * 2 + half], sem, xy * 2 + k, t * 2 + half)
        return jnp.logical_and(differ == 0, k == half), far, near

    def s_copy(c):
        return remote(ssend.at[c], sbuf.at[c, z], s_send.at[c], s_recv.at[c * 2 + z], xy * 2 + k, lax.rem(t + 1, 4) * 2)

    from_a = lax.rem(t + differ * (2 + z), 4)
    from_b = lax.rem(t + 2 - differ + differ * z, 4)

    def collect(c):
        for h in range(2):
            arrived(obuf.at[c, h], o_recv.at[c * 2 + h])
        scale = sc_ref[c]
        for part in range(2):
            o_ref[part, c] = (obuf[c, 0, part].astype(F32) + obuf[c, 1, part].astype(F32)) * scale

        @pl.when(jnp.logical_and(t > 0, k == 0))
        def _():
            for h in range(2):
                arrived(sbuf.at[c, h], s_recv.at[c * 2 + h])
            late = (sbuf[c, 0].astype(F32) + sbuf[c, 1].astype(F32)) * scale
            for part in range(2):
                o_ref[part, c, :SPILL] += late[part * SPILL : (part + 1) * SPILL]

    @pl.loop(0, 8)
    def _(c):
        for slot in (from_a * 2, from_a * 2 + 1, from_b * 2, from_b * 2 + 1):
            arrived(wbuf.at[c, :, w_columns(slot)], w_recv.at[c * 8 + slot])

        def sums(left):
            by_re = lax.dot_general(left, wbuf[c, :BEAMS], NT, preferred_element_type=F32)
            by_im = lax.dot_general(left, wbuf[c, BEAMS:], NT, preferred_element_type=F32)
            n = left.shape[0] // 2
            return (by_re[:n] - by_im[n:]).astype(BF16), (by_re[n:] + by_im[:n]).astype(BF16)

        for half in range(2):
            left = jnp.concatenate(
                [spec[c, half * 128 : half * 128 + 128], spec[c, 256 + half * 128 : 384 + half * 128]], axis=0
            )
            osend[c, half, 0], osend[c, half, 1] = sums(left)
            here, far, near = o_copies(c, half)
            pl.when(here)(near.start)
            pl.when(jnp.logical_not(here))(far.start)
        ssend[c, :SPILL], ssend[c, SPILL:] = sums(spec[c, 512:ROWS])

        @pl.when(t < 3)
        def _():
            s_copy(c).start()

        @pl.when(c > 0)
        def _():
            collect(c - 1)

    collect(7)

    @pl.loop(0, 8)
    def _(c):
        near, sibling, far = w_copies(c)
        for copy in far:
            copy.wait_send()
        always, crossed = forwards(c)
        for copy in always:
            copy.wait_send()

        @pl.when(differ == 1)
        def _():
            sibling.wait_send()
            for copy in crossed:
                copy.wait_send()

        for e in range(2):
            here, far, near = g_copies(c, e)
            pl.when(jnp.logical_not(here))(far.wait_send)
            for k2 in range(2):
                here, far, near = v_copies(c, e, k2)
                pl.when(jnp.logical_not(here))(far.wait_send)
        for half in range(2):
            here, far, near = o_copies(c, half)
            pl.when(jnp.logical_not(here))(far.wait_send)

        @pl.when(t < 3)
        def _():
            s_copy(c).wait_send()


def shards(voltages, channel_gains, weights, scales, fir_taps):
    volts = voltages.reshape(2, INPUTS_HERE, 32, GROUP, SPAN)
    gains = channel_gains.reshape(2 * INPUTS_HERE, 32 * GROUP).T.reshape(32, GROUP, 2 * INPUTS_HERE)
    vmem = pl.BlockSpec(memory_space=pltpu.VMEM)
    dma = pltpu.SemaphoreType.DMA
    formed = pl.pallas_call(
        kernel,
        out_shape=jax.ShapeDtypeStruct((2, GROUP, SPAN, BEAMS), F32),
        in_specs=[
            pl.BlockSpec(memory_space=pl.ANY),
            vmem,
            vmem,
            vmem,
            vmem,
            pl.BlockSpec(memory_space=pltpu.SMEM),
        ],
        out_specs=vmem,
        scratch_shapes=[
            pltpu.VMEM((16, 2, 2, INPUTS_HERE, GROUP, SPAN), BF16),
            pltpu.VMEM((16, GROUP, 2 * INPUTS_HERE), F32),
            pltpu.VMEM((2, GROUP, 2 * BEAMS, 128), BF16),
            pltpu.VMEM((GROUP, 2 * BEAMS, 1024), BF16),
            pltpu.VMEM((GROUP, ROWS, 1024), BF16),
            pltpu.VMEM((2, 1024, 128), F32),
            pltpu.VMEM((1024, 256), BF16),
            pltpu.VMEM((4, 2 * SPILL, 256), F32),
            pltpu.VMEM((GROUP, 2, 2, SPAN, BEAMS), BF16),
            pltpu.VMEM((GROUP, 2, 2, SPAN, BEAMS), BF16),
            pltpu.VMEM((GROUP, 2 * SPILL, BEAMS), BF16),
            pltpu.VMEM((GROUP, 2, 2 * SPILL, BEAMS), BF16),
            dma((32,)),
            dma((32,)),
            dma((16,)),
            dma((16,)),
            dma((40,)),
            dma((64,)),
            dma((32,)),
            dma((16,)),
            dma((16,)),
            dma((8,)),
            dma((16,)),
        ],
        compiler_params=pltpu.CompilerParams(
            collective_id=0, has_side_effects=True, vmem_limit_bytes=58 * 1024 * 1024
        ),
        cost_estimate=pl.CostEstimate(flops=20_000_000_000, bytes_accessed=15_000_000, transcendentals=0),
    )(volts, gains, weights, channelizer(fir_taps), parity_split(), scales)
    return formed.reshape(2, GROUP, SPAN // LENGTH, LENGTH, BEAMS)


def solution(mesh):
    in_specs = (
        P(None, "chan", None, "tm"),
        P(None, "chan", None),
        P(None, "chan", None, "tm"),
        P("chan"),
        P(),
    )
    out_specs = P(None, "chan", "tm", None, None)
    return jax.shard_map(shards, mesh=mesh, in_specs=in_specs, out_specs=out_specs, check_vma=False)
```

```python
import math

import jax
import jax.numpy as jnp
import ml_dtypes
import numpy as np
from jax import lax
from jax.experimental import pallas as pl
from jax.experimental.pallas import tpu as pltpu
from jax.sharding import PartitionSpec as P

MESH = pl.DeviceIdType.MESH
F32 = jnp.float32
BF16 = jnp.bfloat16
NT = (((1,), (1,)), ((), ()))

INPUTS_HERE = 64
GROUP = 8
SPAN = 128
BEAMS = 256
LENGTH = 16
SPILL = 48
ROWS = 4 * SPAN + 2 * SPILL


FRAMES = SPAN // LENGTH
LEAD = 8
SHIFTED = 3

NEAR = [(1, 0), (3, 0), (0, 1), (0, 3)]
FAR = [[(2, 0), (0, 2)], [(1, 1), (3, 3)], [(1, 3), (3, 1)], [(2, 1), (1, 2), (2, 3), (3, 2)], [(2, 2)]]
TARGETS = [(0, 0, 0), (0, 0, 1)] + [(dx, dy, dk) for run in [NEAR] + FAR for dk in range(2) for dx, dy in run]


def turns():
    product = np.arange(LENGTH)[:, None] * (np.arange(SPAN)[None, :] % LENGTH) % LENGTH
    angle = product * (2.0 * math.pi / LENGTH)
    norm = 1.0 / (16.0 * math.sqrt(LENGTH))
    return jnp.asarray(np.stack([np.cos(angle) * norm, np.sin(angle) * norm]).astype(np.float32))


def parity_split():
    q = np.arange(256)
    source = (q % 128) // 64 * 128 + (q // 128) * 64 + q % 64
    return jnp.asarray((np.arange(256)[:, None] == source[None, :]).astype(ml_dtypes.bfloat16))


def kernel(
    v_ref, g_ref, w_ref, turn_ref, perm_ref, taps_ref, sc_ref, o_ref,
    ct, gt, vbuf, gbuf, wsplit, wbuf, spec, vf, xbuf, spf, osend, obuf, ssend, sbuf,
    v_send, v_recv, g_send, g_recv, w_send, w_recv, f_send, o_send, o_recv, s_send, s_recv,
):
    chan, tm = lax.axis_index("chan"), lax.axis_index("tm")
    xy, z = lax.div(chan, 2), lax.rem(chan, 2)
    t, k = lax.div(tm, 2), lax.rem(tm, 2)
    x, y = lax.div(xy, 4), lax.rem(xy, 4)
    u = lax.div(y, 2)
    differ = lax.rem(z + k, 2)

    def remote(src, dst, send, recv, to_chan, to_tm):
        return pltpu.make_async_remote_copy(
            src_ref=src, dst_ref=dst, send_sem=send, recv_sem=recv,
            device_id=(to_chan, to_tm), device_id_type=MESH,
        )

    def arrived(ref, sem):
        pltpu.make_async_copy(ref, ref, sem).wait()

    barrier = pltpu.get_barrier_semaphore()

    @pl.loop(1, 32)
    def _(n):
        other = lax.rem(xy * 2 + k + n, 32)
        pl.semaphore_signal(
            barrier, inc=1, device_id=(lax.div(other, 2) * 2 + z, t * 2 + lax.rem(other, 2)), device_id_type=MESH
        )

    @pl.loop(2, 16)
    def _(n):
        there = lax.rem(t * 2 + z + lax.div(n, 2), 8)
        pl.semaphore_signal(
            barrier, inc=1, device_id=(xy * 2 + lax.rem(there, 2), lax.div(there, 2) * 2 + lax.rem(n, 2)), device_id_type=MESH
        )

    for n in range(2):
        gt[n * 16 : (n + 1) * 16] = g_ref[:, n * 128 : (n + 1) * 128].T.reshape(16, GROUP, 2 * INPUTS_HERE)
    lane = lax.broadcasted_iota(jnp.int32, (LENGTH, SPAN), 1)
    phase, frame = lax.rem(lane, LENGTH), lax.div(lane, LENGTH)
    taps = []
    for tap in range(4):
        values = jnp.zeros((LENGTH, SPAN), F32)
        for n in range(LENGTH):
            values = jnp.where(phase == n, taps_ref[tap, n].astype(F32), values)
        taps.append(values)
    cos, sin = turn_ref[0], turn_ref[1]
    for m in range(FRAMES + 3):
        taken = jnp.zeros((LENGTH, SPAN), F32)
        for tap in range(4):
            taken = jnp.where(frame == m - tap, taps[tap], taken)
        at_re, at_im = (m * 16, SPAN + m * 16) if m < FRAMES else (128 + m * 16, 128 + SPILL + m * 16)
        for at, left, right in ((at_re, cos * taken, sin * taken), (at_im, -sin * taken, cos * taken)):
            full = jnp.concatenate([left, right], axis=1)
            ct[at : at + 16] = full.astype(BF16)
            ct[352 + at : 368 + at] = (full - ct[at : at + 16].astype(F32)).astype(BF16)

    @pl.loop(0, 8)
    def _(c):
        both = jnp.concatenate([w_ref[0, c], w_ref[1, c]], axis=0)
        split = jnp.dot(both, perm_ref[...], preferred_element_type=F32).astype(BF16)
        wsplit[0, c] = split[:, :128]
        wsplit[1, c] = split[:, 128:]

    pl.semaphore_wait(barrier, 31 + 14)

    def v_copy(dx, dy, dk):
        to_xy = lax.rem(x + dx, 4) * 4 + lax.rem(y + dy, 4)
        to_k = lax.rem(k + dk, 2)
        group = to_xy * 2 + to_k
        src, dst, sem = v_ref.at[:, :, group], vbuf.at[xy, k], v_recv.at[xy * 2 + k]
        if (dx, dy, dk) == (0, 0, 0):
            return pltpu.make_async_copy(src, dst, sem)
        return remote(src, dst, v_send.at[group], sem, to_xy * 2 + z, t * 2 + to_k)

    def g_copy(dx, dy):
        to_xy = lax.rem(x + dx, 4) * 4 + lax.rem(y + dy, 4)
        src, dst, sem = gt.at[to_xy * 2 + k], gbuf.at[xy], g_recv.at[xy]
        if (dx, dy) == (0, 0):
            return pltpu.make_async_copy(src, dst, sem)
        return remote(src, dst, g_send.at[to_xy], sem, to_xy * 2 + z, tm)

    def w_columns(slot):
        return pl.ds(pl.multiple_of(slot * 128, 128), 128)

    def w_near(c):
        return pltpu.make_async_copy(wsplit.at[z, c], wbuf.at[c, :, w_columns(tm)], w_recv.at[c * 8 + tm])

    def w_copy(c, index):
        mine, others = wsplit.at[z, c], wsplit.at[1 - z, c]
        over = xy * 2 + 1 - z
        src, to_chan, to_t = [
            (mine, chan, t),
            (others, over, lax.rem(t + z, 4)),
            (others, over, lax.rem(t + z + 3, 4)),
            (mine, chan, lax.rem(t + 1, 4)),
            (mine, chan, lax.rem(t + 3, 4)),
        ][index]
        return remote(
            src, wbuf.at[c, :, w_columns(tm)], w_send.at[c * 5 + index], w_recv.at[c * 8 + tm], to_chan, to_t * 2 + z
        )

    def send_weights(c):
        for index in range(1, 5):
            w_copy(c, index).start()

        @pl.when(differ == 0)
        def _():
            w_near(c).start()

        @pl.when(differ == 1)
        def _():
            w_copy(c, 0).start()

    behind = lax.rem(t + 3 + differ * z, 4)
    ahead = lax.rem(t + 1 - differ + differ * z, 4)

    def forward(c, slot, index, step):
        block = wbuf.at[c, :, w_columns(slot)]
        return remote(
            block, block, f_send.at[c * 4 + index], w_recv.at[c * 8 + slot], chan, lax.rem(t + 4 + step, 4) * 2 + k
        )

    def forwards(c):
        shift = (1 - differ) * (1 - lax.div(c + 8 - SHIFTED, 8))
        return [
            lambda: forward(c, (behind + shift * (ahead - behind)) * 2, 0, 1 - 2 * shift),
            lambda: forward(c, ahead * 2 + 1, 1, -1),
        ]

    def crossed(c):
        return [lambda: forward(c, behind * 2 + 1, 2, 1), lambda: forward(c, ahead * 2, 3, -1)]

    def pass_on(c):
        for slot in (behind * 2, behind * 2 + 1, ahead * 2, ahead * 2 + 1):
            arrived(wbuf.at[c, :, w_columns(slot)], w_recv.at[c * 8 + slot])
        for copy in forwards(c):
            copy().start()

        @pl.when(differ == 1)
        def _():
            for copy in crossed(c):
                copy().start()

        @pl.when(c + LEAD < 8)
        def _():
            send_weights(c + LEAD)

    @pl.loop(0, LEAD)
    def _(c):
        send_weights(c)

    for dx, dy, dk in TARGETS:
        if dk == 0:
            g_copy(dx, dy).start()
        v_copy(dx, dy, dk).start()

    @pl.loop(0, 8)
    def _(p):
        m = lax.div(p + 2, 4)
        odd = lax.rem(p, 2)
        dx = m + lax.rem(m, 2) * 2 * odd
        du = (1 - lax.rem(m, 2)) * odd + lax.rem(m, 2) * lax.div(p, 4)
        pair = lax.rem(x + dx, 4) * 2 + lax.rem(u + du, 2)
        for e in range(2):
            arrived(gbuf.at[pair * 2 + e], g_recv.at[pair * 2 + e])
            for half in range(2):
                arrived(vbuf.at[pair * 2 + e, half], v_recv.at[pair * 4 + 2 * e + half])
        turned = [gbuf[pair * 2 + e].T for e in range(2)]
        gain_re = jnp.concatenate([turned[e][:64] for e in range(2)], axis=0)
        gain_im = jnp.concatenate([turned[e][64:] for e in range(2)], axis=0)
        columns = pl.ds(pl.multiple_of(pair * 128, 128), 128)
        for half in range(2):
            for part in range(2):
                for e in range(2):
                    vf[part, e * 512 : (e + 1) * 512] = (
                        vbuf[pair * 2 + e, half, part].astype(F32).reshape(512, 128)
                    )
            for c in range(8):
                volt_re, volt_im = (
                    jnp.concatenate(
                        [vf.at[part][pl.ds(e * 512 + c, 64, stride=8), :] for e in range(2)], axis=0
                    )
                    for part in range(2)
                )
                g_re, g_im = gain_re[:, c : c + 1], gain_im[:, c : c + 1]
                xbuf[c * 128 : (c + 1) * 128, :128] = (g_re * volt_re - g_im * volt_im).astype(BF16)
                xbuf[c * 128 : (c + 1) * 128, 128:] = (g_re * volt_im + g_im * volt_re).astype(BF16)

            @pl.loop(0, 4)
            def _(q):
                rows = xbuf[pl.ds(pl.multiple_of(q * 256, 256), 256)]
                made = lax.dot_general(ct[...], rows, NT, preferred_element_type=F32)
                made = made[:352] + made[352:]
                re, im, tail = made[:128], made[128:256], made[256:]
                if half == 0:
                    spf[q] = tail
                else:
                    before = spf[q]
                    re = jnp.concatenate([re[:SPILL] + before[:SPILL], re[SPILL:]], axis=0)
                    im = jnp.concatenate([im[:SPILL] + before[SPILL:], im[SPILL:]], axis=0)
                for d in range(2):
                    lanes = slice(d * 128, (d + 1) * 128)
                    spec[q * 2 + d, half * 128 : half * 128 + 128, columns] = re[:, lanes].astype(BF16)
                    spec[q * 2 + d, 256 + half * 128 : 384 + half * 128, columns] = im[:, lanes].astype(BF16)
                    if half == 1:
                        spec[q * 2 + d, 512:ROWS, columns] = tail[:, lanes].astype(BF16)

        @pl.when(p < 6)
        def _():
            pass_on(p)

    def o_copies(c, half):
        src, dst, sem = osend.at[c, half], obuf.at[c, z], o_recv.at[c * 2 + z]
        here = jnp.logical_and(differ == 0, k == half)
        return (
            here,
            lambda: remote(src, dst, o_send.at[c * 2 + half], sem, xy * 2 + k, t * 2 + half),
            lambda: pltpu.make_async_copy(src, dst, sem),
        )

    def s_copy(c):
        return remote(ssend.at[c], sbuf.at[c, z], s_send.at[c], s_recv.at[c * 2 + z], xy * 2 + k, lax.rem(t + 1, 4) * 2)

    from_a = lax.rem(t + differ * (2 + z), 4)
    from_b = lax.rem(t + 2 - differ + differ * z, 4)

    def collect(c):
        for h in range(2):
            arrived(obuf.at[c, h], o_recv.at[c * 2 + h])
        scale = sc_ref[c]
        for part in range(2):
            o_ref[part, c] = (obuf[c, 0, part].astype(F32) + obuf[c, 1, part].astype(F32)) * scale

        @pl.when(jnp.logical_and(t > 0, k == 0))
        def _():
            for h in range(2):
                arrived(sbuf.at[c, h], s_recv.at[c * 2 + h])
            late = (sbuf[c, 0].astype(F32) + sbuf[c, 1].astype(F32)) * scale
            for part in range(2):
                o_ref[part, c, :SPILL] += late[part * SPILL : (part + 1) * SPILL]

    @pl.loop(0, 8)
    def _(c):
        for slot in (from_a * 2, from_a * 2 + 1, from_b * 2, from_b * 2 + 1):
            arrived(wbuf.at[c, :, w_columns(slot)], w_recv.at[c * 8 + slot])

        def sums(left):
            by_re = lax.dot_general(left, wbuf[c, :BEAMS], NT, preferred_element_type=F32)
            by_im = lax.dot_general(left, wbuf[c, BEAMS:], NT, preferred_element_type=F32)
            n = left.shape[0] // 2
            return (by_re[:n] - by_im[n:]).astype(BF16), (by_re[n:] + by_im[:n]).astype(BF16)

        for half in range(2):
            left = jnp.concatenate(
                [spec[c, half * 128 : half * 128 + 128], spec[c, 256 + half * 128 : 384 + half * 128]], axis=0
            )
            osend[c, half, 0], osend[c, half, 1] = sums(left)
            here, far, near = o_copies(c, half)
            pl.when(here)(lambda near=near: near().start())
            pl.when(jnp.logical_not(here))(lambda far=far: far().start())
        ssend[c, :SPILL], ssend[c, SPILL:] = sums(spec[c, 512:ROWS])

        @pl.when(t < 3)
        def _():
            s_copy(c).start()

        @pl.when(c > 0)
        def _():
            collect(c - 1)

        @pl.when(lax.rem(c, 3) == 2)
        def _():
            pass_on(6 + lax.div(c - 2, 3))

    collect(7)

    for dx, dy, dk in TARGETS[1:]:
        v_copy(dx, dy, dk).wait_send()
        if dk == 0:
            g_copy(dx, dy).wait_send()

    @pl.loop(0, 8)
    def _(c):
        for index in range(1, 5):
            w_copy(c, index).wait_send()
        for copy in forwards(c):
            copy().wait_send()

        @pl.when(differ == 1)
        def _():
            w_copy(c, 0).wait_send()
            for copy in crossed(c):
                copy().wait_send()

        for half in range(2):
            here, far, near = o_copies(c, half)
            pl.when(jnp.logical_not(here))(lambda far=far: far().wait_send())

        @pl.when(t < 3)
        def _():
            s_copy(c).wait_send()


def shards(voltages, channel_gains, weights, scales, fir_taps):
    volts = voltages.reshape(2, INPUTS_HERE, 32, GROUP, SPAN)
    gains = channel_gains.reshape(2 * INPUTS_HERE, 32 * GROUP)
    vmem = pl.BlockSpec(memory_space=pltpu.VMEM)
    dma = pltpu.SemaphoreType.DMA
    formed = pl.pallas_call(
        kernel,
        out_shape=jax.ShapeDtypeStruct((2, GROUP, SPAN, BEAMS), F32),
        in_specs=[
            pl.BlockSpec(memory_space=pl.ANY),
            vmem,
            vmem,
            vmem,
            vmem,
            pl.BlockSpec(memory_space=pltpu.SMEM),
            pl.BlockSpec(memory_space=pltpu.SMEM),
        ],
        out_specs=vmem,
        scratch_shapes=[
            pltpu.VMEM((704, 256), BF16),
            pltpu.VMEM((32, GROUP, 2 * INPUTS_HERE), F32),
            pltpu.VMEM((16, 2, 2, INPUTS_HERE, GROUP, SPAN), BF16),
            pltpu.VMEM((16, GROUP, 2 * INPUTS_HERE), F32),
            pltpu.VMEM((2, GROUP, 2 * BEAMS, 128), BF16),
            pltpu.VMEM((GROUP, 2 * BEAMS, 1024), BF16),
            pltpu.VMEM((GROUP, ROWS, 1024), BF16),
            pltpu.VMEM((2, 1024, 128), F32),
            pltpu.VMEM((1024, 256), BF16),
            pltpu.VMEM((4, 2 * SPILL, 256), F32),
            pltpu.VMEM((GROUP, 2, 2, SPAN, BEAMS), BF16),
            pltpu.VMEM((GROUP, 2, 2, SPAN, BEAMS), BF16),
            pltpu.VMEM((GROUP, 2 * SPILL, BEAMS), BF16),
            pltpu.VMEM((GROUP, 2, 2 * SPILL, BEAMS), BF16),
            dma((32,)),
            dma((32,)),
            dma((16,)),
            dma((16,)),
            dma((40,)),
            dma((64,)),
            dma((32,)),
            dma((16,)),
            dma((16,)),
            dma((8,)),
            dma((16,)),
        ],
        compiler_params=pltpu.CompilerParams(
            collective_id=0, has_side_effects=True, vmem_limit_bytes=58 * 1024 * 1024
        ),
        cost_estimate=pl.CostEstimate(flops=20_000_000_000, bytes_accessed=15_000_000, transcendentals=0),
    )(volts, gains, weights, turns(), parity_split(), fir_taps, scales)
    return formed.reshape(2, GROUP, SPAN // LENGTH, LENGTH, BEAMS)


def solution(mesh):
    in_specs = (
        P(None, "chan", None, "tm"),
        P(None, "chan", None),
        P(None, "chan", None, "tm"),
        P("chan"),
        P(),
    )
    out_specs = P(None, "chan", "tm", None, None)
    return jax.shard_map(shards, mesh=mesh, in_specs=in_specs, out_specs=out_specs, check_vma=False)
```

```python
import math

import jax
import jax.numpy as jnp
import ml_dtypes
import numpy as np
from jax import lax
from jax.experimental import pallas as pl
from jax.experimental.pallas import tpu as pltpu
from jax.sharding import PartitionSpec as P

MESH = pl.DeviceIdType.MESH
F32 = jnp.float32
BF16 = jnp.bfloat16
NT = (((1,), (1,)), ((), ()))

INPUTS_HERE = 64
GROUP = 8
SPAN = 128
BEAMS = 256
LENGTH = 16
SPILL = 48
ROWS = 4 * SPAN + 2 * SPILL


FRAMES = SPAN // LENGTH
PASSED = [(0, 3), (3, 8)]
SHIFTED = 1

RUNS = [
    [(2, 1), (0, 3), (2, 3), (0, 1)],
    [(1, 2), (3, 0), (3, 2), (1, 0)],
    [(1, 1), (3, 3)],
    [(1, 3), (3, 1)],
    [(2, 0), (0, 2)],
    [(2, 2)],
]
TARGETS = [(0, 0, 0), (0, 0, 1)] + [(dx, dy, dk) for run in RUNS for dx, dy in run for dk in range(2)]


def turns():
    product = np.arange(LENGTH)[:, None] * (np.arange(SPAN)[None, :] % LENGTH) % LENGTH
    angle = product * (2.0 * math.pi / LENGTH)
    norm = 1.0 / (16.0 * math.sqrt(LENGTH))
    return jnp.asarray(np.stack([np.cos(angle) * norm, np.sin(angle) * norm]).astype(np.float32))


def parity_split():
    q = np.arange(256)
    source = (q % 128) // 64 * 128 + (q // 128) * 64 + q % 64
    return jnp.asarray((np.arange(256)[:, None] == source[None, :]).astype(ml_dtypes.bfloat16))


def kernel(
    v_ref, g_ref, w_ref, turn_ref, perm_ref, taps_ref, sc_ref, o_ref,
    wv, ct, gt, vbuf, gbuf, wsplit, wbuf, spec, vf, xbuf, spf, osend, obuf, ssend, sbuf,
    v_send, v_recv, g_send, g_recv, w_load, w_send, w_recv, f_send, o_send, o_recv, s_send, s_recv,
):
    chan, tm = lax.axis_index("chan"), lax.axis_index("tm")
    xy, z = lax.div(chan, 2), lax.rem(chan, 2)
    t, k = lax.div(tm, 2), lax.rem(tm, 2)
    x, y = lax.div(xy, 4), lax.rem(xy, 4)
    u = lax.div(y, 2)
    differ = lax.rem(z + k, 2)

    def remote(src, dst, send, recv, to_chan, to_tm):
        return pltpu.make_async_remote_copy(
            src_ref=src, dst_ref=dst, send_sem=send, recv_sem=recv,
            device_id=(to_chan, to_tm), device_id_type=MESH,
        )

    def arrived(ref, sem):
        pltpu.make_async_copy(ref, ref, sem).wait()

    pltpu.make_async_copy(w_ref, wv, w_load).start()

    barrier = pltpu.get_barrier_semaphore()

    @pl.loop(1, 32)
    def _(n):
        other = lax.rem(xy * 2 + k + n, 32)
        pl.semaphore_signal(
            barrier, inc=1, device_id=(lax.div(other, 2) * 2 + z, t * 2 + lax.rem(other, 2)), device_id_type=MESH
        )

    @pl.loop(2, 16)
    def _(n):
        there = lax.rem(t * 2 + z + lax.div(n, 2), 8)
        pl.semaphore_signal(
            barrier, inc=1, device_id=(xy * 2 + lax.rem(there, 2), lax.div(there, 2) * 2 + lax.rem(n, 2)), device_id_type=MESH
        )

    def split(c):
        both = jnp.concatenate([wv[0, c], wv[1, c]], axis=0)
        turned = jnp.dot(both, perm_ref[...], preferred_element_type=F32).astype(BF16)
        wsplit[0, c] = turned[:, :128]
        wsplit[1, c] = turned[:, 128:]

    pltpu.make_async_copy(w_ref, wv, w_load).wait()
    split(0)
    pl.semaphore_wait(barrier, 31 + 14)

    def v_copy(dx, dy, dk):
        to_xy = lax.rem(x + dx, 4) * 4 + lax.rem(y + dy, 4)
        to_k = lax.rem(k + dk, 2)
        group = to_xy * 2 + to_k
        src, dst, sem = v_ref.at[:, :, group], vbuf.at[xy, k], v_recv.at[xy * 2 + k]
        if (dx, dy, dk) == (0, 0, 0):
            return pltpu.make_async_copy(src, dst, sem)
        return remote(src, dst, v_send.at[group], sem, to_xy * 2 + z, t * 2 + to_k)

    def g_copy(dx, dy):
        to_xy = lax.rem(x + dx, 4) * 4 + lax.rem(y + dy, 4)
        src, dst, sem = gt.at[to_xy * 2 + k], gbuf.at[xy], g_recv.at[xy]
        if (dx, dy) == (0, 0):
            return pltpu.make_async_copy(src, dst, sem)
        return remote(src, dst, g_send.at[to_xy], sem, to_xy * 2 + z, tm)

    def w_columns(slot):
        return pl.ds(pl.multiple_of(slot * 128, 128), 128)

    def w_near(c):
        return pltpu.make_async_copy(wsplit.at[z, c], wbuf.at[c, :, w_columns(tm)], w_recv.at[c * 8 + tm])

    def w_copy(c, index):
        mine, others = wsplit.at[z, c], wsplit.at[1 - z, c]
        over = xy * 2 + 1 - z
        src, to_chan, to_t = [
            (mine, chan, t),
            (others, over, lax.rem(t + z, 4)),
            (others, over, lax.rem(t + z + 3, 4)),
            (mine, chan, lax.rem(t + 1, 4)),
            (mine, chan, lax.rem(t + 3, 4)),
        ][index]
        return remote(
            src, wbuf.at[c, :, w_columns(tm)], w_send.at[c * 5 + index], w_recv.at[c * 8 + tm], to_chan, to_t * 2 + z
        )

    def send_weights(c):
        for index in range(1, 5):
            w_copy(c, index).start()

        @pl.when(differ == 0)
        def _():
            w_near(c).start()

        @pl.when(differ == 1)
        def _():
            w_copy(c, 0).start()

    behind = lax.rem(t + 3 + differ * z, 4)
    ahead = lax.rem(t + 1 - differ + differ * z, 4)

    def forward(c, slot, index, step):
        block = wbuf.at[c, :, w_columns(slot)]
        return remote(
            block, block, f_send.at[c * 4 + index], w_recv.at[c * 8 + slot], chan, lax.rem(t + 4 + step, 4) * 2 + k
        )

    def forwards(c):
        shift = (1 - differ) * (1 - lax.div(c + 8 - SHIFTED, 8))
        return [
            lambda: forward(c, (behind + shift * (ahead - behind)) * 2, 0, 1 - 2 * shift),
            lambda: forward(c, ahead * 2 + 1, 1, -1),
        ]

    def crossed(c):
        return [lambda: forward(c, behind * 2 + 1, 2, 1), lambda: forward(c, ahead * 2, 3, -1)]

    def pass_on(c):
        for slot in (behind * 2, behind * 2 + 1, ahead * 2, ahead * 2 + 1):
            arrived(wbuf.at[c, :, w_columns(slot)], w_recv.at[c * 8 + slot])
        for copy in forwards(c):
            copy().start()

        @pl.when(differ == 1)
        def _():
            for copy in crossed(c):
                copy().start()

    send_weights(0)
    for dx, dy, dk in TARGETS:
        v_copy(dx, dy, dk).start()

    @pl.loop(1, 8)
    def _(c):
        split(c)
        send_weights(c)

    for n in range(2):
        gt[n * 16 : (n + 1) * 16] = g_ref[:, n * 128 : (n + 1) * 128].T.reshape(16, GROUP, 2 * INPUTS_HERE)
    for dx, dy, dk in TARGETS:
        if dk == 0:
            g_copy(dx, dy).start()

    lane = lax.broadcasted_iota(jnp.int32, (LENGTH, SPAN), 1)
    phase, frame = lax.rem(lane, LENGTH), lax.div(lane, LENGTH)
    taps = []
    for tap in range(4):
        values = jnp.zeros((LENGTH, SPAN), F32)
        for n in range(LENGTH):
            values = jnp.where(phase == n, taps_ref[tap, n].astype(F32), values)
        taps.append(values)
    cos, sin = turn_ref[0], turn_ref[1]
    for m in range(FRAMES + 3):
        taken = jnp.zeros((LENGTH, SPAN), F32)
        for tap in range(4):
            taken = jnp.where(frame == m - tap, taps[tap], taken)
        at_re, at_im = (m * 16, SPAN + m * 16) if m < FRAMES else (128 + m * 16, 128 + SPILL + m * 16)
        for at, left, right in ((at_re, cos * taken, sin * taken), (at_im, -sin * taken, cos * taken)):
            full = jnp.concatenate([left, right], axis=1)
            ct[at : at + 16] = full.astype(BF16)
            ct[352 + at : 368 + at] = (full - ct[at : at + 16].astype(F32)).astype(BF16)

    @pl.loop(0, 8)
    def _(p):
        for step, (first, last) in enumerate(PASSED):
            pl.when(p == step)(lambda first=first, last=last: pl.loop(first, last)(pass_on))

        m = lax.rem(lax.div(p + 3, 4), 2)
        dx = m * (3 - 2 * lax.rem(p, 2)) + 2 * lax.div(p, 6)
        du = lax.rem(lax.div(p, 3) + lax.div(p, 7), 2)
        pair = lax.rem(x + dx, 4) * 2 + lax.rem(u + du, 2)
        for e in range(2):
            arrived(gbuf.at[pair * 2 + e], g_recv.at[pair * 2 + e])
            for half in range(2):
                arrived(vbuf.at[pair * 2 + e, half], v_recv.at[pair * 4 + 2 * e + half])
        turned = [gbuf[pair * 2 + e].T for e in range(2)]
        gain_re = jnp.concatenate([turned[e][:64] for e in range(2)], axis=0)
        gain_im = jnp.concatenate([turned[e][64:] for e in range(2)], axis=0)
        columns = pl.ds(pl.multiple_of(pair * 128, 128), 128)
        for half in range(2):
            for part in range(2):
                for e in range(2):
                    vf[part, e * 512 : (e + 1) * 512] = (
                        vbuf[pair * 2 + e, half, part].astype(F32).reshape(512, 128)
                    )
            for c in range(8):
                volt_re, volt_im = (
                    jnp.concatenate(
                        [vf.at[part][pl.ds(e * 512 + c, 64, stride=8), :] for e in range(2)], axis=0
                    )
                    for part in range(2)
                )
                g_re, g_im = gain_re[:, c : c + 1], gain_im[:, c : c + 1]
                xbuf[c * 128 : (c + 1) * 128, :128] = (g_re * volt_re - g_im * volt_im).astype(BF16)
                xbuf[c * 128 : (c + 1) * 128, 128:] = (g_re * volt_im + g_im * volt_re).astype(BF16)

            @pl.loop(0, 4)
            def _(q):
                rows = xbuf[pl.ds(pl.multiple_of(q * 256, 256), 256)]
                made = lax.dot_general(ct[...], rows, NT, preferred_element_type=F32)
                made = made[:352] + made[352:]
                re, im, tail = made[:128], made[128:256], made[256:]
                if half == 0:
                    spf[q] = tail
                else:
                    before = spf[q]
                    re = jnp.concatenate([re[:SPILL] + before[:SPILL], re[SPILL:]], axis=0)
                    im = jnp.concatenate([im[:SPILL] + before[SPILL:], im[SPILL:]], axis=0)
                for d in range(2):
                    lanes = slice(d * 128, (d + 1) * 128)
                    spec[q * 2 + d, half * 128 : half * 128 + 128, columns] = re[:, lanes].astype(BF16)
                    spec[q * 2 + d, 256 + half * 128 : 384 + half * 128, columns] = im[:, lanes].astype(BF16)
                    if half == 1:
                        spec[q * 2 + d, 512:ROWS, columns] = tail[:, lanes].astype(BF16)

    def o_copies(c, half):
        src, dst, sem = osend.at[c, half], obuf.at[c, z], o_recv.at[c * 2 + z]
        here = jnp.logical_and(differ == 0, k == half)
        return (
            here,
            lambda: remote(src, dst, o_send.at[c * 2 + half], sem, xy * 2 + k, t * 2 + half),
            lambda: pltpu.make_async_copy(src, dst, sem),
        )

    def s_copy(c):
        return remote(ssend.at[c], sbuf.at[c, z], s_send.at[c], s_recv.at[c * 2 + z], xy * 2 + k, lax.rem(t + 1, 4) * 2)

    from_a = lax.rem(t + differ * (2 + z), 4)
    from_b = lax.rem(t + 2 - differ + differ * z, 4)

    def collect(c):
        for h in range(2):
            arrived(obuf.at[c, h], o_recv.at[c * 2 + h])
        scale = sc_ref[c]
        for part in range(2):
            o_ref[part, c] = (obuf[c, 0, part].astype(F32) + obuf[c, 1, part].astype(F32)) * scale

        @pl.when(jnp.logical_and(t > 0, k == 0))
        def _():
            for h in range(2):
                arrived(sbuf.at[c, h], s_recv.at[c * 2 + h])
            late = (sbuf[c, 0].astype(F32) + sbuf[c, 1].astype(F32)) * scale
            for part in range(2):
                o_ref[part, c, :SPILL] += late[part * SPILL : (part + 1) * SPILL]

    @pl.loop(0, 8)
    def _(c):
        for slot in (from_a * 2, from_a * 2 + 1, from_b * 2, from_b * 2 + 1):
            arrived(wbuf.at[c, :, w_columns(slot)], w_recv.at[c * 8 + slot])

        def sums(left):
            by_re = lax.dot_general(left, wbuf[c, :BEAMS], NT, preferred_element_type=F32)
            by_im = lax.dot_general(left, wbuf[c, BEAMS:], NT, preferred_element_type=F32)
            n = left.shape[0] // 2
            return (by_re[:n] - by_im[n:]).astype(BF16), (by_re[n:] + by_im[:n]).astype(BF16)

        ssend[c, :SPILL], ssend[c, SPILL:] = sums(spec[c, 512:ROWS])

        @pl.when(t < 3)
        def _():
            s_copy(c).start()

        for half in range(2):
            left = jnp.concatenate(
                [spec[c, half * 128 : half * 128 + 128], spec[c, 256 + half * 128 : 384 + half * 128]], axis=0
            )
            osend[c, half, 0], osend[c, half, 1] = sums(left)
            here, far, near = o_copies(c, half)
            pl.when(here)(lambda near=near: near().start())
            pl.when(jnp.logical_not(here))(lambda far=far: far().start())

        @pl.when(c > 0)
        def _():
            collect(c - 1)


    collect(7)

    for dx, dy, dk in TARGETS[1:]:
        v_copy(dx, dy, dk).wait_send()
        if dk == 0:
            g_copy(dx, dy).wait_send()

    @pl.loop(0, 8)
    def _(c):
        for index in range(1, 5):
            w_copy(c, index).wait_send()
        for copy in forwards(c):
            copy().wait_send()

        @pl.when(differ == 1)
        def _():
            w_copy(c, 0).wait_send()
            for copy in crossed(c):
                copy().wait_send()

        for half in range(2):
            here, far, near = o_copies(c, half)
            pl.when(jnp.logical_not(here))(lambda far=far: far().wait_send())

        @pl.when(t < 3)
        def _():
            s_copy(c).wait_send()


def shards(voltages, channel_gains, weights, scales, fir_taps):
    volts = voltages.reshape(2, INPUTS_HERE, 32, GROUP, SPAN)
    gains = channel_gains.reshape(2 * INPUTS_HERE, 32 * GROUP)
    vmem = pl.BlockSpec(memory_space=pltpu.VMEM)
    dma = pltpu.SemaphoreType.DMA
    formed = pl.pallas_call(
        kernel,
        out_shape=jax.ShapeDtypeStruct((2, GROUP, SPAN, BEAMS), F32),
        in_specs=[
            pl.BlockSpec(memory_space=pl.ANY),
            vmem,
            pl.BlockSpec(memory_space=pl.ANY),
            vmem,
            vmem,
            pl.BlockSpec(memory_space=pltpu.SMEM),
            pl.BlockSpec(memory_space=pltpu.SMEM),
        ],
        out_specs=vmem,
        scratch_shapes=[
            pltpu.VMEM((2, GROUP, BEAMS, 256), BF16),
            pltpu.VMEM((704, 256), BF16),
            pltpu.VMEM((32, GROUP, 2 * INPUTS_HERE), F32),
            pltpu.VMEM((16, 2, 2, INPUTS_HERE, GROUP, SPAN), BF16),
            pltpu.VMEM((16, GROUP, 2 * INPUTS_HERE), F32),
            pltpu.VMEM((2, GROUP, 2 * BEAMS, 128), BF16),
            pltpu.VMEM((GROUP, 2 * BEAMS, 1024), BF16),
            pltpu.VMEM((GROUP, ROWS, 1024), BF16),
            pltpu.VMEM((2, 1024, 128), F32),
            pltpu.VMEM((1024, 256), BF16),
            pltpu.VMEM((4, 2 * SPILL, 256), F32),
            pltpu.VMEM((GROUP, 2, 2, SPAN, BEAMS), BF16),
            pltpu.VMEM((GROUP, 2, 2, SPAN, BEAMS), BF16),
            pltpu.VMEM((GROUP, 2 * SPILL, BEAMS), BF16),
            pltpu.VMEM((GROUP, 2, 2 * SPILL, BEAMS), BF16),
            dma((32,)),
            dma((32,)),
            dma((16,)),
            dma((16,)),
            dma,
            dma((40,)),
            dma((64,)),
            dma((32,)),
            dma((16,)),
            dma((16,)),
            dma((8,)),
            dma((16,)),
        ],
        compiler_params=pltpu.CompilerParams(
            collective_id=0, has_side_effects=True, vmem_limit_bytes=58 * 1024 * 1024
        ),
        cost_estimate=pl.CostEstimate(flops=20_000_000_000, bytes_accessed=15_000_000, transcendentals=0),
    )(volts, gains, weights, turns(), parity_split(), fir_taps, scales)
    return formed.reshape(2, GROUP, SPAN // LENGTH, LENGTH, BEAMS)


def solution(mesh):
    in_specs = (
        P(None, "chan", None, "tm"),
        P(None, "chan", None),
        P(None, "chan", None, "tm"),
        P("chan"),
        P(),
    )
    out_specs = P(None, "chan", "tm", None, None)
    return jax.shard_map(shards, mesh=mesh, in_specs=in_specs, out_specs=out_specs, check_vma=False)
```

```python
import math

import jax
import jax.numpy as jnp
import ml_dtypes
import numpy as np
from jax import lax
from jax.experimental import pallas as pl
from jax.experimental.pallas import tpu as pltpu
from jax.sharding import PartitionSpec as P

MESH = pl.DeviceIdType.MESH
F32 = jnp.float32
BF16 = jnp.bfloat16
NT = (((1,), (1,)), ((), ()))

INPUTS_HERE = 64
GROUP = 8
SPAN = 128
BEAMS = 256
LENGTH = 16
SPILL = 48
ROWS = 4 * SPAN + 2 * SPILL


FRAMES = SPAN // LENGTH
PASSED = [(0, 3), (3, 8)]

RUNS = [
    [(2, 1), (0, 3), (2, 3), (0, 1)],
    [(1, 2), (3, 0), (3, 2), (1, 0)],
    [(1, 1), (3, 3)],
    [(1, 3), (3, 1)],
    [(2, 0), (0, 2)],
    [(2, 2)],
]
TARGETS = [(0, 0, 0), (0, 0, 1)] + [(dx, dy, dk) for run in RUNS for dx, dy in run for dk in range(2)]


def turns():
    product = np.arange(LENGTH)[:, None] * (np.arange(SPAN)[None, :] % LENGTH) % LENGTH
    angle = product * (2.0 * math.pi / LENGTH)
    norm = 1.0 / (16.0 * math.sqrt(LENGTH))
    return jnp.asarray(np.stack([np.cos(angle) * norm, np.sin(angle) * norm]).astype(np.float32))


def parity_split():
    q = np.arange(256)
    source = (q % 128) // 64 * 128 + (q // 128) * 64 + q % 64
    return jnp.asarray((np.arange(256)[:, None] == source[None, :]).astype(ml_dtypes.bfloat16))


def kernel(
    v_ref, g_ref, w_ref, turn_ref, perm_ref, taps_ref, sc_ref, o_ref,
    wv, ct, gt, vbuf, gbuf, wsplit, wbuf, spec, vf, xbuf, spf, osend, obuf, ssend, sbuf,
    v_send, v_recv, g_send, g_recv, w_load, w_send, w_recv, f_send, o_send, o_recv, s_send, s_recv,
):
    chan, tm = lax.axis_index("chan"), lax.axis_index("tm")
    xy, z = lax.div(chan, 2), lax.rem(chan, 2)
    t, k = lax.div(tm, 2), lax.rem(tm, 2)
    x, y = lax.div(xy, 4), lax.rem(xy, 4)
    u = lax.div(y, 2)
    differ = lax.rem(z + k, 2)

    def remote(src, dst, send, recv, to_chan, to_tm):
        return pltpu.make_async_remote_copy(
            src_ref=src, dst_ref=dst, send_sem=send, recv_sem=recv,
            device_id=(to_chan, to_tm), device_id_type=MESH,
        )

    def arrived(ref, sem):
        pltpu.make_async_copy(ref, ref, sem).wait()

    pltpu.make_async_copy(w_ref, wv, w_load).start()

    barrier = pltpu.get_barrier_semaphore()

    @pl.loop(1, 32)
    def _(n):
        other = lax.rem(xy * 2 + k + n, 32)
        pl.semaphore_signal(
            barrier, inc=1, device_id=(lax.div(other, 2) * 2 + z, t * 2 + lax.rem(other, 2)), device_id_type=MESH
        )

    @pl.loop(2, 16)
    def _(n):
        there = lax.rem(t * 2 + z + lax.div(n, 2), 8)
        pl.semaphore_signal(
            barrier, inc=1, device_id=(xy * 2 + lax.rem(there, 2), lax.div(there, 2) * 2 + lax.rem(n, 2)), device_id_type=MESH
        )

    def split(c):
        both = jnp.concatenate([wv[0, c], wv[1, c]], axis=0)
        turned = jnp.dot(both, perm_ref[...], preferred_element_type=F32).astype(BF16)
        wsplit[0, c] = turned[:, :128]
        wsplit[1, c] = turned[:, 128:]

    pltpu.make_async_copy(w_ref, wv, w_load).wait()
    split(0)
    pl.semaphore_wait(barrier, 31 + 14)

    def v_copy(dx, dy, dk):
        to_xy = lax.rem(x + dx, 4) * 4 + lax.rem(y + dy, 4)
        to_k = lax.rem(k + dk, 2)
        group = to_xy * 2 + to_k
        src, dst, sem = v_ref.at[:, :, group], vbuf.at[xy, k], v_recv.at[xy * 2 + k]
        if (dx, dy, dk) == (0, 0, 0):
            return pltpu.make_async_copy(src, dst, sem)
        return remote(src, dst, v_send.at[group], sem, to_xy * 2 + z, t * 2 + to_k)

    def g_copy(dx, dy):
        to_xy = lax.rem(x + dx, 4) * 4 + lax.rem(y + dy, 4)
        src, dst, sem = gt.at[to_xy * 2 + k], gbuf.at[xy], g_recv.at[xy]
        if (dx, dy) == (0, 0):
            return pltpu.make_async_copy(src, dst, sem)
        return remote(src, dst, g_send.at[to_xy], sem, to_xy * 2 + z, tm)

    def w_columns(slot):
        return pl.ds(pl.multiple_of(slot * 128, 128), 128)

    def w_near(c):
        return pltpu.make_async_copy(wsplit.at[z, c], wbuf.at[c, :, w_columns(tm)], w_recv.at[c * 8 + tm])

    def w_copy(c, index):
        mine, others = wsplit.at[z, c], wsplit.at[1 - z, c]
        over = xy * 2 + 1 - z
        src, to_chan, to_t = [
            (mine, chan, t),
            (others, over, lax.rem(t + z, 4)),
            (others, over, lax.rem(t + z + 3, 4)),
            (mine, chan, lax.rem(t + 1, 4)),
            (mine, chan, lax.rem(t + 3, 4)),
        ][index]
        return remote(
            src, wbuf.at[c, :, w_columns(tm)], w_send.at[c * 5 + index], w_recv.at[c * 8 + tm], to_chan, to_t * 2 + z
        )

    def send_weights(c):
        for index in range(1, 5):
            w_copy(c, index).start()

        @pl.when(differ == 0)
        def _():
            w_near(c).start()

        @pl.when(differ == 1)
        def _():
            w_copy(c, 0).start()

    behind = lax.rem(t + 3 + differ * z, 4)
    ahead = lax.rem(t + 1 - differ + differ * z, 4)

    def forward(c, slot, index, step):
        block = wbuf.at[c, :, w_columns(slot)]
        return remote(
            block, block, f_send.at[c * 4 + index], w_recv.at[c * 8 + slot], chan, lax.rem(t + 4 + step, 4) * 2 + k
        )

    def forwards(c):
        return [
            lambda: forward(c, behind * 2, 0, 1),
            lambda: forward(c, ahead * 2 + 1, 1, -1),
        ]

    def crossed(c):
        return [lambda: forward(c, behind * 2 + 1, 2, 1), lambda: forward(c, ahead * 2, 3, -1)]

    def pass_on(c):
        for slot in (behind * 2, behind * 2 + 1, ahead * 2, ahead * 2 + 1):
            arrived(wbuf.at[c, :, w_columns(slot)], w_recv.at[c * 8 + slot])
        for copy in forwards(c):
            copy().start()

        @pl.when(differ == 1)
        def _():
            for copy in crossed(c):
                copy().start()

    send_weights(0)
    for dx, dy, dk in TARGETS:
        v_copy(dx, dy, dk).start()

    @pl.loop(1, 8)
    def _(c):
        split(c)
        send_weights(c)

    for n in range(2):
        gt[n * 16 : (n + 1) * 16] = g_ref[:, n * 128 : (n + 1) * 128].T.reshape(16, GROUP, 2 * INPUTS_HERE)
    for dx, dy, dk in TARGETS:
        if dk == 0:
            g_copy(dx, dy).start()

    lane = lax.broadcasted_iota(jnp.int32, (LENGTH, SPAN), 1)
    phase, frame = lax.rem(lane, LENGTH), lax.div(lane, LENGTH)
    taps = []
    for tap in range(4):
        values = jnp.zeros((LENGTH, SPAN), F32)
        for n in range(LENGTH):
            values = jnp.where(phase == n, taps_ref[tap, n].astype(F32), values)
        taps.append(values)
    cos, sin = turn_ref[0], turn_ref[1]
    for m in range(FRAMES + 3):
        taken = jnp.zeros((LENGTH, SPAN), F32)
        for tap in range(4):
            taken = jnp.where(frame == m - tap, taps[tap], taken)
        at_re, at_im = (m * 16, SPAN + m * 16) if m < FRAMES else (128 + m * 16, 128 + SPILL + m * 16)
        for at, left, right in ((at_re, cos * taken, sin * taken), (at_im, -sin * taken, cos * taken)):
            full = jnp.concatenate([left, right], axis=1)
            ct[at : at + 16] = full.astype(BF16)
            ct[352 + at : 368 + at] = (full - ct[at : at + 16].astype(F32)).astype(BF16)

    @pl.loop(0, 8)
    def _(p):
        for step, (first, last) in enumerate(PASSED):
            pl.when(p == step)(lambda first=first, last=last: pl.loop(first, last)(pass_on))

        m = lax.rem(lax.div(p + 3, 4), 2)
        dx = m * (3 - 2 * lax.rem(p, 2)) + 2 * lax.div(p, 6)
        du = lax.rem(lax.div(p, 3) + lax.div(p, 7), 2)
        pair = lax.rem(x + dx, 4) * 2 + lax.rem(u + du, 2)
        for e in range(2):
            arrived(gbuf.at[pair * 2 + e], g_recv.at[pair * 2 + e])
            for half in range(2):
                arrived(vbuf.at[pair * 2 + e, half], v_recv.at[pair * 4 + 2 * e + half])
        turned = [gbuf[pair * 2 + e].T for e in range(2)]
        gain_re = jnp.concatenate([turned[e][:64] for e in range(2)], axis=0)
        gain_im = jnp.concatenate([turned[e][64:] for e in range(2)], axis=0)
        columns = pl.ds(pl.multiple_of(pair * 128, 128), 128)
        for half in range(2):
            for part in range(2):
                for e in range(2):
                    vf[part, e * 512 : (e + 1) * 512] = (
                        vbuf[pair * 2 + e, half, part].astype(F32).reshape(512, 128)
                    )
            for c in range(8):
                volt_re, volt_im = (
                    jnp.concatenate(
                        [vf.at[part][pl.ds(e * 512 + c, 64, stride=8), :] for e in range(2)], axis=0
                    )
                    for part in range(2)
                )
                g_re, g_im = gain_re[:, c : c + 1], gain_im[:, c : c + 1]
                xbuf[c * 128 : (c + 1) * 128, :128] = (g_re * volt_re - g_im * volt_im).astype(BF16)
                xbuf[c * 128 : (c + 1) * 128, 128:] = (g_re * volt_im + g_im * volt_re).astype(BF16)

            @pl.loop(0, 4)
            def _(q):
                rows = xbuf[pl.ds(pl.multiple_of(q * 256, 256), 256)]
                made = lax.dot_general(ct[...], rows, NT, preferred_element_type=F32)
                made = made[:352] + made[352:]
                re, im, tail = made[:128], made[128:256], made[256:]
                if half == 0:
                    spf[q] = tail
                else:
                    before = spf[q]
                    re = jnp.concatenate([re[:SPILL] + before[:SPILL], re[SPILL:]], axis=0)
                    im = jnp.concatenate([im[:SPILL] + before[SPILL:], im[SPILL:]], axis=0)
                for d in range(2):
                    lanes = slice(d * 128, (d + 1) * 128)
                    spec[q * 2 + d, half * 128 : half * 128 + 128, columns] = re[:, lanes].astype(BF16)
                    spec[q * 2 + d, 256 + half * 128 : 384 + half * 128, columns] = im[:, lanes].astype(BF16)
                    if half == 1:
                        spec[q * 2 + d, 512:ROWS, columns] = tail[:, lanes].astype(BF16)

    def o_copies(c, half):
        src, dst, sem = osend.at[c, half], obuf.at[c, z], o_recv.at[c * 2 + z]
        here = jnp.logical_and(differ == 0, k == half)
        return (
            here,
            lambda: remote(src, dst, o_send.at[c * 2 + half], sem, xy * 2 + k, t * 2 + half),
            lambda: pltpu.make_async_copy(src, dst, sem),
        )

    def s_copy(c):
        return remote(ssend.at[c], sbuf.at[c, z], s_send.at[c], s_recv.at[c * 2 + z], xy * 2, lax.rem(t + 1, 4) * 2 + k)

    from_a = lax.rem(t + differ * (2 + z), 4)
    from_b = lax.rem(t + 2 - differ + differ * z, 4)

    def collect(c):
        for h in range(2):
            arrived(obuf.at[c, h], o_recv.at[c * 2 + h])
        scale = sc_ref[c]
        for part in range(2):
            o_ref[part, c] = (obuf[c, 0, part].astype(F32) + obuf[c, 1, part].astype(F32)) * scale

    @pl.loop(0, 8)
    def _(c):
        for slot in (from_a * 2, from_a * 2 + 1, from_b * 2, from_b * 2 + 1):
            arrived(wbuf.at[c, :, w_columns(slot)], w_recv.at[c * 8 + slot])

        def sums(left):
            by_re = lax.dot_general(left, wbuf[c, :BEAMS], NT, preferred_element_type=F32)
            by_im = lax.dot_general(left, wbuf[c, BEAMS:], NT, preferred_element_type=F32)
            n = left.shape[0] // 2
            return by_re[:n] - by_im[n:], by_re[n:] + by_im[:n]

        for part, values in enumerate(sums(spec[c, 512:ROWS])):
            ssend[c, part * SPILL : (part + 1) * SPILL] = values.astype(BF16)

        @pl.when(t < 3)
        def _():
            s_copy(c).start()

        for half in (1, 0):
            left = jnp.concatenate(
                [spec[c, half * 128 : half * 128 + 128], spec[c, 256 + half * 128 : 384 + half * 128]], axis=0
            )
            formed = sums(left)
            for part in range(2):
                osend[c, half, part] = formed[part].astype(BF16)
            if half == 0:
                @pl.when(jnp.logical_and(t > 0, z == 0))
                def _():
                    for h in range(2):
                        arrived(sbuf.at[c, h], s_recv.at[c * 2 + h])
                    for part in range(2):
                        rows = slice(part * SPILL, (part + 1) * SPILL)
                        late = sbuf[c, 0, rows].astype(F32) + sbuf[c, 1, rows].astype(F32)
                        osend[c, 0, part, :SPILL] = (formed[part][:SPILL] + late).astype(BF16)

            here, far, near = o_copies(c, half)
            pl.when(here)(lambda near=near: near().start())
            pl.when(jnp.logical_not(here))(lambda far=far: far().start())

        @pl.when(c > 0)
        def _():
            collect(c - 1)


    collect(7)

    for dx, dy, dk in TARGETS[1:]:
        v_copy(dx, dy, dk).wait_send()
        if dk == 0:
            g_copy(dx, dy).wait_send()

    @pl.loop(0, 8)
    def _(c):
        for index in range(1, 5):
            w_copy(c, index).wait_send()
        for copy in forwards(c):
            copy().wait_send()

        @pl.when(differ == 1)
        def _():
            w_copy(c, 0).wait_send()
            for copy in crossed(c):
                copy().wait_send()

        for half in range(2):
            here, far, near = o_copies(c, half)
            pl.when(jnp.logical_not(here))(lambda far=far: far().wait_send())

        @pl.when(t < 3)
        def _():
            s_copy(c).wait_send()


def shards(voltages, channel_gains, weights, scales, fir_taps):
    volts = voltages.reshape(2, INPUTS_HERE, 32, GROUP, SPAN)
    gains = channel_gains.reshape(2 * INPUTS_HERE, 32 * GROUP)
    vmem = pl.BlockSpec(memory_space=pltpu.VMEM)
    dma = pltpu.SemaphoreType.DMA
    formed = pl.pallas_call(
        kernel,
        out_shape=jax.ShapeDtypeStruct((2, GROUP, SPAN, BEAMS), F32),
        in_specs=[
            pl.BlockSpec(memory_space=pl.ANY),
            vmem,
            pl.BlockSpec(memory_space=pl.ANY),
            vmem,
            vmem,
            pl.BlockSpec(memory_space=pltpu.SMEM),
            pl.BlockSpec(memory_space=pltpu.SMEM),
        ],
        out_specs=vmem,
        scratch_shapes=[
            pltpu.VMEM((2, GROUP, BEAMS, 256), BF16),
            pltpu.VMEM((704, 256), BF16),
            pltpu.VMEM((32, GROUP, 2 * INPUTS_HERE), F32),
            pltpu.VMEM((16, 2, 2, INPUTS_HERE, GROUP, SPAN), BF16),
            pltpu.VMEM((16, GROUP, 2 * INPUTS_HERE), F32),
            pltpu.VMEM((2, GROUP, 2 * BEAMS, 128), BF16),
            pltpu.VMEM((GROUP, 2 * BEAMS, 1024), BF16),
            pltpu.VMEM((GROUP, ROWS, 1024), BF16),
            pltpu.VMEM((2, 1024, 128), F32),
            pltpu.VMEM((1024, 256), BF16),
            pltpu.VMEM((4, 2 * SPILL, 256), F32),
            pltpu.VMEM((GROUP, 2, 2, SPAN, BEAMS), BF16),
            pltpu.VMEM((GROUP, 2, 2, SPAN, BEAMS), BF16),
            pltpu.VMEM((GROUP, 2 * SPILL, BEAMS), BF16),
            pltpu.VMEM((GROUP, 2, 2 * SPILL, BEAMS), BF16),
            dma((32,)),
            dma((32,)),
            dma((16,)),
            dma((16,)),
            dma,
            dma((40,)),
            dma((64,)),
            dma((32,)),
            dma((16,)),
            dma((16,)),
            dma((8,)),
            dma((16,)),
        ],
        compiler_params=pltpu.CompilerParams(
            collective_id=0, has_side_effects=True, vmem_limit_bytes=58 * 1024 * 1024
        ),
        cost_estimate=pl.CostEstimate(flops=20_000_000_000, bytes_accessed=15_000_000, transcendentals=0),
    )(volts, gains, weights, turns(), parity_split(), fir_taps, scales)
    return formed.reshape(2, GROUP, SPAN // LENGTH, LENGTH, BEAMS)


def solution(mesh):
    in_specs = (
        P(None, "chan", None, "tm"),
        P(None, "chan", None),
        P(None, "chan", None, "tm"),
        P("chan"),
        P(),
    )
    out_specs = P(None, "chan", "tm", None, None)
    return jax.shard_map(shards, mesh=mesh, in_specs=in_specs, out_specs=out_specs, check_vma=False)
```

```python
import math

import jax
import jax.numpy as jnp
import ml_dtypes
import numpy as np
from jax import lax
from jax.experimental import pallas as pl
from jax.experimental.pallas import tpu as pltpu
from jax.sharding import PartitionSpec as P

MESH = pl.DeviceIdType.MESH
F32 = jnp.float32
BF16 = jnp.bfloat16
NT = (((1,), (1,)), ((), ()))

INPUTS_HERE = 64
GROUP = 8
SPAN = 128
BEAMS = 256
LENGTH = 16
SPILL = 48
ROWS = 4 * SPAN + 2 * SPILL


FRAMES = SPAN // LENGTH
PASSED = [(0, 3), (3, 8)]

RUNS = [
    [(2, 1), (0, 3), (2, 3), (0, 1)],
    [(1, 2), (3, 0), (3, 2), (1, 0)],
    [(1, 1), (3, 3)],
    [(1, 3), (3, 1)],
    [(2, 0), (0, 2)],
    [(2, 2)],
]
TARGETS = [(0, 0, 0), (0, 0, 1)] + [(dx, dy, dk) for run in RUNS for dx, dy in run for dk in range(2)]


def turns():
    product = np.arange(LENGTH)[:, None] * (np.arange(SPAN)[None, :] % LENGTH) % LENGTH
    angle = product * (2.0 * math.pi / LENGTH)
    norm = 1.0 / (16.0 * math.sqrt(LENGTH))
    return jnp.asarray(np.stack([np.cos(angle) * norm, np.sin(angle) * norm]).astype(np.float32))


def parity_split():
    q = np.arange(256)
    source = (q % 128) // 64 * 128 + (q // 128) * 64 + q % 64
    return jnp.asarray((np.arange(256)[:, None] == source[None, :]).astype(ml_dtypes.bfloat16))


def kernel(
    v_ref, g_ref, w_ref, turn_ref, perm_ref, taps_ref, sc_ref, o_ref,
    wv, ct, gt, vbuf, gbuf, wsplit, wbuf, spec, vf, xbuf, spf, osend, obuf, ssend, sbuf,
    v_send, v_recv, g_send, g_recv, w_load, w_send, w_recv, f_send, o_send, o_recv, s_send, s_recv,
):
    chan, tm = lax.axis_index("chan"), lax.axis_index("tm")
    xy, z = lax.div(chan, 2), lax.rem(chan, 2)
    t, k = lax.div(tm, 2), lax.rem(tm, 2)
    x, y = lax.div(xy, 4), lax.rem(xy, 4)
    u = lax.div(y, 2)
    differ = lax.rem(z + k, 2)

    def remote(src, dst, send, recv, to_chan, to_tm):
        return pltpu.make_async_remote_copy(
            src_ref=src, dst_ref=dst, send_sem=send, recv_sem=recv,
            device_id=(to_chan, to_tm), device_id_type=MESH,
        )

    def arrived(ref, sem):
        pltpu.make_async_copy(ref, ref, sem).wait()

    pltpu.make_async_copy(w_ref, wv, w_load).start()

    barrier = pltpu.get_barrier_semaphore()

    @pl.loop(1, 32)
    def _(n):
        other = lax.rem(xy * 2 + k + n, 32)
        pl.semaphore_signal(
            barrier, inc=1, device_id=(lax.div(other, 2) * 2 + z, t * 2 + lax.rem(other, 2)), device_id_type=MESH
        )

    @pl.loop(2, 16)
    def _(n):
        there = lax.rem(t * 2 + z + lax.div(n, 2), 8)
        pl.semaphore_signal(
            barrier, inc=1, device_id=(xy * 2 + lax.rem(there, 2), lax.div(there, 2) * 2 + lax.rem(n, 2)), device_id_type=MESH
        )

    def split(c):
        both = jnp.concatenate([wv[0, c], wv[1, c]], axis=0)
        turned = jnp.dot(both, perm_ref[...], preferred_element_type=F32).astype(BF16)
        wsplit[0, c] = turned[:, :128]
        wsplit[1, c] = turned[:, 128:]

    pltpu.make_async_copy(w_ref, wv, w_load).wait()
    split(0)
    split(1)
    pl.semaphore_wait(barrier, 31 + 14)

    def v_copy(dx, dy, dk):
        to_xy = lax.rem(x + dx, 4) * 4 + lax.rem(y + dy, 4)
        to_k = lax.rem(k + dk, 2)
        group = to_xy * 2 + to_k
        src, dst, sem = v_ref.at[:, :, group], vbuf.at[xy, k], v_recv.at[xy * 2 + k]
        if (dx, dy, dk) == (0, 0, 0):
            return pltpu.make_async_copy(src, dst, sem)
        return remote(src, dst, v_send.at[group], sem, to_xy * 2 + z, t * 2 + to_k)

    def g_copy(dx, dy):
        to_xy = lax.rem(x + dx, 4) * 4 + lax.rem(y + dy, 4)
        src, dst, sem = gt.at[to_xy * 2 + k], gbuf.at[xy], g_recv.at[xy]
        if (dx, dy) == (0, 0):
            return pltpu.make_async_copy(src, dst, sem)
        return remote(src, dst, g_send.at[to_xy], sem, to_xy * 2 + z, tm)

    def w_columns(slot):
        return pl.ds(pl.multiple_of(slot * 128, 128), 128)

    def w_near(c):
        return pltpu.make_async_copy(wsplit.at[z, c], wbuf.at[c, :, w_columns(tm)], w_recv.at[c * 8 + tm])

    def w_copy(c, index):
        mine, others = wsplit.at[z, c], wsplit.at[1 - z, c]
        over = xy * 2 + 1 - z
        src, to_chan, to_t = [
            (mine, chan, t),
            (others, over, lax.rem(t + z, 4)),
            (others, over, lax.rem(t + z + 3, 4)),
            (mine, chan, lax.rem(t + 1, 4)),
            (mine, chan, lax.rem(t + 3, 4)),
        ][index]
        return remote(
            src, wbuf.at[c, :, w_columns(tm)], w_send.at[c * 5 + index], w_recv.at[c * 8 + tm], to_chan, to_t * 2 + z
        )

    def send_weights(c):
        for index in range(1, 5):
            w_copy(c, index).start()

        @pl.when(differ == 0)
        def _():
            w_near(c).start()

        @pl.when(differ == 1)
        def _():
            w_copy(c, 0).start()

    behind = lax.rem(t + 3 + differ * z, 4)
    ahead = lax.rem(t + 1 - differ + differ * z, 4)

    def forward(c, slot, index, step):
        block = wbuf.at[c, :, w_columns(slot)]
        return remote(
            block, block, f_send.at[c * 4 + index], w_recv.at[c * 8 + slot], chan, lax.rem(t + 4 + step, 4) * 2 + k
        )

    def forwards(c):
        return [
            lambda: forward(c, behind * 2, 0, 1),
            lambda: forward(c, ahead * 2 + 1, 1, -1),
        ]

    def crossed(c):
        return [lambda: forward(c, behind * 2 + 1, 2, 1), lambda: forward(c, ahead * 2, 3, -1)]

    def pass_on(c):
        for slot in (behind * 2, behind * 2 + 1, ahead * 2, ahead * 2 + 1):
            arrived(wbuf.at[c, :, w_columns(slot)], w_recv.at[c * 8 + slot])
        for copy in forwards(c):
            copy().start()

        @pl.when(differ == 1)
        def _():
            for copy in crossed(c):
                copy().start()

    send_weights(0)
    send_weights(1)
    for dx, dy, dk in TARGETS:
        v_copy(dx, dy, dk).start()

    @pl.loop(2, 8)
    def _(c):
        split(c)
        send_weights(c)

    for n in range(2):
        gt[n * 16 : (n + 1) * 16] = g_ref[:, n * 128 : (n + 1) * 128].T.reshape(16, GROUP, 2 * INPUTS_HERE)
    for dx, dy, dk in TARGETS:
        if dk == 0:
            g_copy(dx, dy).start()

    lane = lax.broadcasted_iota(jnp.int32, (LENGTH, SPAN), 1)
    phase, frame = lax.rem(lane, LENGTH), lax.div(lane, LENGTH)
    taps = []
    for tap in range(4):
        values = jnp.zeros((LENGTH, SPAN), F32)
        for n in range(LENGTH):
            values = jnp.where(phase == n, taps_ref[tap, n].astype(F32), values)
        taps.append(values)
    cos, sin = turn_ref[0], turn_ref[1]
    for m in range(FRAMES + 3):
        taken = jnp.zeros((LENGTH, SPAN), F32)
        for tap in range(4):
            taken = jnp.where(frame == m - tap, taps[tap], taken)
        at_re, at_im = (m * 16, SPAN + m * 16) if m < FRAMES else (128 + m * 16, 128 + SPILL + m * 16)
        for at, left, right in ((at_re, cos * taken, sin * taken), (at_im, -sin * taken, cos * taken)):
            full = jnp.concatenate([left, right], axis=1)
            ct[at : at + 16] = full.astype(BF16)
            ct[352 + at : 368 + at] = (full - ct[at : at + 16].astype(F32)).astype(BF16)

    @pl.loop(0, 8)
    def _(p):
        for step, (first, last) in enumerate(PASSED):
            pl.when(p == step)(lambda first=first, last=last: pl.loop(first, last)(pass_on))

        m = lax.rem(lax.div(p + 3, 4), 2)
        dx = m * (3 - 2 * lax.rem(p, 2)) + 2 * lax.div(p, 6)
        du = lax.rem(lax.div(p, 3) + lax.div(p, 7), 2)
        pair = lax.rem(x + dx, 4) * 2 + lax.rem(u + du, 2)
        for e in range(2):
            arrived(gbuf.at[pair * 2 + e], g_recv.at[pair * 2 + e])
            for half in range(2):
                arrived(vbuf.at[pair * 2 + e, half], v_recv.at[pair * 4 + 2 * e + half])
        turned = [gbuf[pair * 2 + e].T for e in range(2)]
        gain_re = jnp.concatenate([turned[e][:64] for e in range(2)], axis=0)
        gain_im = jnp.concatenate([turned[e][64:] for e in range(2)], axis=0)
        columns = pl.ds(pl.multiple_of(pair * 128, 128), 128)
        for half in range(2):
            for part in range(2):
                for e in range(2):
                    vf[part, e * 512 : (e + 1) * 512] = (
                        vbuf[pair * 2 + e, half, part].astype(F32).reshape(512, 128)
                    )
            for c in range(8):
                volt_re, volt_im = (
                    jnp.concatenate(
                        [vf.at[part][pl.ds(e * 512 + c, 64, stride=8), :] for e in range(2)], axis=0
                    )
                    for part in range(2)
                )
                g_re, g_im = gain_re[:, c : c + 1], gain_im[:, c : c + 1]
                xbuf[c * 128 : (c + 1) * 128, :128] = (g_re * volt_re - g_im * volt_im).astype(BF16)
                xbuf[c * 128 : (c + 1) * 128, 128:] = (g_re * volt_im + g_im * volt_re).astype(BF16)

            @pl.loop(0, 4)
            def _(q):
                rows = xbuf[pl.ds(pl.multiple_of(q * 256, 256), 256)]
                made = lax.dot_general(ct[...], rows, NT, preferred_element_type=F32)
                made = made[:352] + made[352:]
                re, im, tail = made[:128], made[128:256], made[256:]
                if half == 0:
                    spf[q] = tail
                else:
                    before = spf[q]
                    re = jnp.concatenate([re[:SPILL] + before[:SPILL], re[SPILL:]], axis=0)
                    im = jnp.concatenate([im[:SPILL] + before[SPILL:], im[SPILL:]], axis=0)
                for d in range(2):
                    lanes = slice(d * 128, (d + 1) * 128)
                    spec[q * 2 + d, half * 128 : half * 128 + 128, columns] = re[:, lanes].astype(BF16)
                    spec[q * 2 + d, 256 + half * 128 : 384 + half * 128, columns] = im[:, lanes].astype(BF16)
                    if half == 1:
                        spec[q * 2 + d, 512:ROWS, columns] = tail[:, lanes].astype(BF16)

    def o_copies(c, half):
        src, dst, sem = osend.at[c, half], obuf.at[c, z], o_recv.at[c * 2 + z]
        here = jnp.logical_and(differ == 0, k == half)
        return (
            here,
            lambda: remote(src, dst, o_send.at[c * 2 + half], sem, xy * 2 + k, t * 2 + half),
            lambda: pltpu.make_async_copy(src, dst, sem),
        )

    def s_copy(c):
        return remote(ssend.at[c], sbuf.at[c, z], s_send.at[c], s_recv.at[c * 2 + z], xy * 2, lax.rem(t + 1, 4) * 2 + k)

    from_a = lax.rem(t + differ * (2 + z), 4)
    from_b = lax.rem(t + 2 - differ + differ * z, 4)

    def collect(c):
        for h in range(2):
            arrived(obuf.at[c, h], o_recv.at[c * 2 + h])
        scale = sc_ref[c]
        for part in range(2):
            o_ref[part, c] = (obuf[c, 0, part].astype(F32) + obuf[c, 1, part].astype(F32)) * scale

    @pl.loop(0, 8)
    def _(c):
        for slot in (from_a * 2, from_a * 2 + 1, from_b * 2, from_b * 2 + 1):
            arrived(wbuf.at[c, :, w_columns(slot)], w_recv.at[c * 8 + slot])

        def sums(left):
            by_re = lax.dot_general(left, wbuf[c, :BEAMS], NT, preferred_element_type=F32)
            by_im = lax.dot_general(left, wbuf[c, BEAMS:], NT, preferred_element_type=F32)
            n = left.shape[0] // 2
            return by_re[:n] - by_im[n:], by_re[n:] + by_im[:n]

        for part, values in enumerate(sums(spec[c, 512:ROWS])):
            ssend[c, part * SPILL : (part + 1) * SPILL] = values.astype(BF16)

        @pl.when(t < 3)
        def _():
            s_copy(c).start()

        for half in (1, 0):
            left = jnp.concatenate(
                [spec[c, half * 128 : half * 128 + 128], spec[c, 256 + half * 128 : 384 + half * 128]], axis=0
            )
            formed = sums(left)
            for part in range(2):
                osend[c, half, part] = formed[part].astype(BF16)
            if half == 0:
                @pl.when(jnp.logical_and(t > 0, z == 0))
                def _():
                    for h in range(2):
                        arrived(sbuf.at[c, h], s_recv.at[c * 2 + h])
                    for part in range(2):
                        rows = slice(part * SPILL, (part + 1) * SPILL)
                        late = sbuf[c, 0, rows].astype(F32) + sbuf[c, 1, rows].astype(F32)
                        osend[c, 0, part, :SPILL] = (formed[part][:SPILL] + late).astype(BF16)

            here, far, near = o_copies(c, half)
            pl.when(here)(lambda near=near: near().start())
            pl.when(jnp.logical_not(here))(lambda far=far: far().start())

        @pl.when(c > 0)
        def _():
            collect(c - 1)


    collect(7)

    for dx, dy, dk in TARGETS[1:]:
        v_copy(dx, dy, dk).wait_send()
        if dk == 0:
            g_copy(dx, dy).wait_send()

    @pl.loop(0, 8)
    def _(c):
        for index in range(1, 5):
            w_copy(c, index).wait_send()
        for copy in forwards(c):
            copy().wait_send()

        @pl.when(differ == 1)
        def _():
            w_copy(c, 0).wait_send()
            for copy in crossed(c):
                copy().wait_send()

        for half in range(2):
            here, far, near = o_copies(c, half)
            pl.when(jnp.logical_not(here))(lambda far=far: far().wait_send())

        @pl.when(t < 3)
        def _():
            s_copy(c).wait_send()


def shards(voltages, channel_gains, weights, scales, fir_taps):
    volts = voltages.reshape(2, INPUTS_HERE, 32, GROUP, SPAN)
    gains = channel_gains.reshape(2 * INPUTS_HERE, 32 * GROUP)
    vmem = pl.BlockSpec(memory_space=pltpu.VMEM)
    dma = pltpu.SemaphoreType.DMA
    formed = pl.pallas_call(
        kernel,
        out_shape=jax.ShapeDtypeStruct((2, GROUP, SPAN, BEAMS), F32),
        in_specs=[
            pl.BlockSpec(memory_space=pl.ANY),
            vmem,
            pl.BlockSpec(memory_space=pl.ANY),
            vmem,
            vmem,
            pl.BlockSpec(memory_space=pltpu.SMEM),
            pl.BlockSpec(memory_space=pltpu.SMEM),
        ],
        out_specs=vmem,
        scratch_shapes=[
            pltpu.VMEM((2, GROUP, BEAMS, 256), BF16),
            pltpu.VMEM((704, 256), BF16),
            pltpu.VMEM((32, GROUP, 2 * INPUTS_HERE), F32),
            pltpu.VMEM((16, 2, 2, INPUTS_HERE, GROUP, SPAN), BF16),
            pltpu.VMEM((16, GROUP, 2 * INPUTS_HERE), F32),
            pltpu.VMEM((2, GROUP, 2 * BEAMS, 128), BF16),
            pltpu.VMEM((GROUP, 2 * BEAMS, 1024), BF16),
            pltpu.VMEM((GROUP, ROWS, 1024), BF16),
            pltpu.VMEM((2, 1024, 128), F32),
            pltpu.VMEM((1024, 256), BF16),
            pltpu.VMEM((4, 2 * SPILL, 256), F32),
            pltpu.VMEM((GROUP, 2, 2, SPAN, BEAMS), BF16),
            pltpu.VMEM((GROUP, 2, 2, SPAN, BEAMS), BF16),
            pltpu.VMEM((GROUP, 2 * SPILL, BEAMS), BF16),
            pltpu.VMEM((GROUP, 2, 2 * SPILL, BEAMS), BF16),
            dma((32,)),
            dma((32,)),
            dma((16,)),
            dma((16,)),
            dma,
            dma((40,)),
            dma((64,)),
            dma((32,)),
            dma((16,)),
            dma((16,)),
            dma((8,)),
            dma((16,)),
        ],
        compiler_params=pltpu.CompilerParams(
            collective_id=0, has_side_effects=True, vmem_limit_bytes=58 * 1024 * 1024
        ),
        cost_estimate=pl.CostEstimate(flops=20_000_000_000, bytes_accessed=15_000_000, transcendentals=0),
    )(volts, gains, weights, turns(), parity_split(), fir_taps, scales)
    return formed.reshape(2, GROUP, SPAN // LENGTH, LENGTH, BEAMS)


def solution(mesh):
    in_specs = (
        P(None, "chan", None, "tm"),
        P(None, "chan", None),
        P(None, "chan", None, "tm"),
        P("chan"),
        P(),
    )
    out_specs = P(None, "chan", "tm", None, None)
    return jax.shard_map(shards, mesh=mesh, in_specs=in_specs, out_specs=out_specs, check_vma=False)
```
